32 devices in a mesh: section: 2 (over y), dp: 4 (over x, core), tensor: 4 (over z).
Axes of the slice: x: 2, y: 2, z: 4, core: 2. Of those that a mesh axis runs over, the one named last changes fastest.
Arguments:
- tokens: bfloat16 [4, 5, 256, 1024], P('dp', None, 'tensor'), may hold values from -6 to 6
- cotangent: float32 [4, 5, 256, 1024], P('dp', None, 'tensor'), may hold values from -6 to 6
- norm_gain: float32 [2, 1024], P('section'), may hold values from 0.5 to 1.5
- gate_weight: bfloat16 [2, 1024, 2048], P('section', 'dp', 'tensor'), may hold values from -0.1875 to 0.1875
- inner_weight: bfloat16 [2, 1024, 2048], P('section', 'dp', 'tensor'), may hold values from -0.1875 to 0.1875
- state_weight: bfloat16 [2, 1024, 256], P('section', 'dp'), may hold values from -0.1875 to 0.1875
- step_weight: bfloat16 [2, 1024, 32], P('section', 'dp', 'tensor'), may hold values from -0.25 to 0.25
- conv_inner: float32 [2, 5, 2048], P('section', None, 'tensor'), may hold values from -3 to 3
- conv_state: float32 [2, 5, 256], P('section'), may hold values from -3 to 3
- head_params: float32 [2, 3, 32], P('section', None, 'tensor'), may hold values from -7 to 1.4, as said below
- gate_gain: float32 [2, 2048], P('section'), may hold values from 0.5 to 1.5
- out_weight: bfloat16 [2, 2048, 1024], P('section', None, 'dp'), may hold values from -0.125 to 0.125
Outputs:
- output: float32 [2, 4, 5, 256, 1024], P('section', 'dp', None, 'tensor')
- input_grad: float32 [2, 4, 5, 256, 1024], P('section', 'dp', None, 'tensor')
- grad_norm_gain: float32 [2, 1024], P('section')
- grad_gate_weight: float32 [2, 1024, 2048], P('section', 'dp', 'tensor')
- grad_inner_weight: float32 [2, 1024, 2048], P('section', 'dp', 'tensor')
- grad_state_weight: float32 [2, 1024, 256], P('section', 'dp')
- grad_step_weight: float32 [2, 1024, 32], P('section', 'dp', 'tensor')
- grad_conv_inner: float32 [2, 5, 2048], P('section', None, 'tensor')
- grad_conv_state: float32 [2, 5, 256], P('section')
- grad_head_params: float32 [2, 3, 32], P('section', None, 'tensor')
- grad_gate_gain: float32 [2, 2048], P('section', 'tensor')
- grad_out_weight: float32 [2, 2048, 1024], P('section', 'tensor', 'dp')
The draws below stay inside these ranges and needn't reach their ends.
Inputs may be any that keep to these rules, and one draw needn't show every extreme that they name: `head_params`: row 0 of each layer is added to the raw step sizes before softplus, row 1 is the logarithm of each head's decay rate, row 2 is each head's skip weight.
All inputs are finite; a program needn't handle non-finite values.
Results may differ from the reference program's by a relative error of at most 0.011.
Values may be sent and summed in bfloat16 or wider, within the bound.
A program may use at most 192 MiB of HBM per device.

```python
import jax
import jax.numpy as jnp
from jax import lax

D = 1024
HEADS = 32
HEADDIM = 64
STATE = 128
CONV = 4
GROUP = 256
MBS = 5
INNER = 2048
SEQS = 4
LEN = 1280
N_SECTION = 2


def draw_head_params(key, part):
    key = jax.random.fold_in(key, 7)
    bias_key, rate_key, skip_key = jax.random.split(key, 3)
    step_bias = jax.random.uniform(bias_key, (2, 1, HEADS), jnp.float32, -6.5, -2.0)
    rate_log = jax.random.uniform(rate_key, (2, 1, HEADS), jnp.float32, -0.7, 1.4)
    skip_gain = jax.random.uniform(skip_key, (2, 1, HEADS), jnp.float32, 0.2, 1.2)
    return jnp.concatenate([step_bias, rate_log, skip_gain], 1)


def spiked(values, key, source, target, parts, factor):
    owner, partner = [(jnp.arange(values.shape[position]) // (values.shape[position] // parts)).reshape([-1 if axis == position else 1 for axis in range(values.ndim)]) for position in (source, target)]
    chosen = jax.random.permutation(key, parts)[partner]
    strong = (owner == chosen) | (owner == (partner + parts // 2) % parts)
    return jnp.where(strong, factor * values, values)


def steps_of(key, shape, shards, low, high):
    factor_of, own = 1.0, jax.random.fold_in(key, 6)
    for axis_at, shards_of in shards:
        heights = jnp.exp(jax.random.uniform(jax.random.fold_in(own, axis_at), (shards_of,), jnp.float32, low / len(shards), high / len(shards)))
        factor_of = factor_of * jnp.repeat(heights, shape[axis_at] // shards_of).reshape([-1 if axis == axis_at else 1 for axis in range(len(shape))])
    return factor_of


def noise(own_key, dims, scale, most, cuts=(), kind=jnp.bfloat16):
    factor_of = steps_of(own_key, dims, cuts, -0.22, 0.18) if cuts else 1.0
    drawn = jax.random.normal(own_key, dims, jnp.float32) * scale * factor_of
    return jnp.minimum(jnp.maximum(drawn, -most), most).astype(kind)


def gaussian_with(own_key, dims, width, reach, cuts, heavy, held_as=jnp.bfloat16):
    values = width * jax.random.normal(own_key, dims, jnp.float32)
    if cuts:
        values = values * steps_of(own_key, dims, cuts, -0.22, 0.18)
    return jnp.clip(spiked(values, jax.random.fold_in(own_key, 3), *heavy), -reach, reach).astype(held_as)


def setup_inputs(seed: int = 0) -> dict:
    streams_of = jax.random.split(jax.random.key(seed), 13)
    tokens = gaussian_with(streams_of[0], (SEQS, MBS, GROUP, D), 1.0, 6.0, ((0, 4), (2, 4)), (0, 3, 4, 2.0))
    cotangent = gaussian_with(streams_of[1], (SEQS, MBS, GROUP, D), 1.0, 6.0, ((0, 4), (2, 4)), (0, 3, 4, 2.0), jnp.float32)
    norm_gain = jnp.clip(1.0 + 0.1 * jax.random.normal(streams_of[2], (N_SECTION, D), jnp.float32), 0.5, 1.5)
    gate_weight = noise(streams_of[3], (N_SECTION, D, INNER), D ** -0.5, 0.1875, ((0, 2), (1, 4), (2, 4)))
    inner_weight = noise(streams_of[4], (N_SECTION, D, INNER), D ** -0.5, 0.1875, ((0, 2), (1, 4), (2, 4)))
    state_weight = noise(streams_of[5], (N_SECTION, D, 2 * STATE), D ** -0.5, 0.1875, ((0, 2), (1, 4)))
    step_weight = noise(streams_of[6], (N_SECTION, D, HEADS), (D // 2) ** -0.5, 0.25, ((0, 2), (1, 4), (2, 4)))
    conv_inner = noise(streams_of[7], (N_SECTION, CONV + 1, INNER), 0.5, 3.0, ((0, 2), (2, 4)), jnp.float32)
    conv_state = noise(streams_of[8], (N_SECTION, CONV + 1, 2 * STATE), 0.5, 3.0, ((0, 2),), jnp.float32)
    head_params = draw_head_params(jax.random.fold_in(streams_of[12], 71), 0)
    gate_gain = jnp.clip(1.0 + 0.1 * jax.random.normal(streams_of[10], (N_SECTION, INNER), jnp.float32), 0.5, 1.5)
    out_weight = noise(streams_of[11], (N_SECTION, INNER, D), INNER ** -0.5, 0.125, ((0, 2), (2, 4)))
    return {"tokens": tokens, "cotangent": cotangent, "norm_gain": norm_gain, "gate_weight": gate_weight, "inner_weight": inner_weight, "state_weight": state_weight, "step_weight": step_weight, "conv_inner": conv_inner, "conv_state": conv_state, "head_params": head_params, "gate_gain": gate_gain, "out_weight": out_weight}


EPSILON = 1e-05
FULL_PRECISION = lax.Precision.HIGHEST

@jax.custom_vjp
def low(v):
    return lax.optimization_barrier(v.astype(jnp.bfloat16)).astype(jnp.float32)

@jax.custom_vjp
def low_back(v):
    return v

def low_keep(v):
    return (low(v), None)

def low_pass(kept, grad):
    return (grad,)

def back_keep(v):
    return (v, None)

def back_low(kept, grad):
    return (low(grad),)
low.defvjp(low_keep, low_pass)
low_back.defvjp(back_keep, back_low)

def causal_conv(padded, tap_rows):
    steps_out = padded.shape[0] - tap_rows.shape[0] + 2
    summed = tap_rows[-1] + jnp.zeros_like(padded[:steps_out])
    for offset in range(tap_rows.shape[0] - 1):
        summed = summed + tap_rows[offset] * padded[offset:offset + steps_out]
    return summed

def ssd_block(x_heads, b_state, c_state, step_size, decay_rate, skip_weight, carried):
    log_decay = step_size * decay_rate
    running = jnp.cumsum(log_decay, axis=0)
    length = running.shape[0]
    by_head = jnp.transpose(running, (1, 2, 0))
    spread = by_head[..., :, None] - by_head[..., None, :]
    causal_mask = lax.broadcasted_iota(jnp.int32, (length, length), 0) >= lax.broadcasted_iota(jnp.int32, (length, length), 1)
    kernel = jnp.where(causal_mask, jnp.exp(jnp.where(causal_mask, spread, 0.0)), 0.0)
    scores_cb = jnp.einsum('tbn,sbn->bts', c_state, b_state, precision=FULL_PRECISION)
    mixing = scores_cb[:, None] * kernel * jnp.transpose(step_size, (1, 2, 0))[:, :, None, :]
    inside = jnp.einsum('bhts,sbhp->tbhp', mixing, x_heads, precision=FULL_PRECISION)
    carried_out = jnp.einsum('tbn,bhpn->tbhp', c_state, carried, precision=FULL_PRECISION) * jnp.exp(running)[..., None]
    outputs = inside + carried_out + skip_weight[:, None] * x_heads
    last_sum = running[-1]
    weighting = jnp.exp(last_sum[None] - running) * step_size
    updated = jnp.exp(last_sum)[..., None, None] * carried + jnp.einsum('sbh,sbhp,sbn->bhpn', weighting, x_heads, b_state, precision=FULL_PRECISION)
    return (outputs, updated)

def mixer_core(projected, step_raw, tail_inner, tail_state, carried, taps_inner, taps_state, head_rows):
    width_loc = taps_inner.shape[1]
    heads_loc = head_rows.shape[1]
    joined_inner = jnp.concatenate([tail_inner, projected[..., width_loc:2 * width_loc]], 0)
    joined_state = jnp.concatenate([tail_state, projected[..., 2 * width_loc:]], 0)
    inner_act = jax.nn.silu(causal_conv(joined_inner, taps_inner))
    state_act = jax.nn.silu(causal_conv(joined_state, taps_state))
    x_heads = inner_act.reshape(inner_act.shape[0], inner_act.shape[1], heads_loc, HEADDIM)
    step_size = jax.nn.softplus(step_raw + head_rows[0])
    head_out, updated = ssd_block(x_heads, state_act[..., :STATE], state_act[..., STATE:], step_size, -jnp.exp(head_rows[1]), head_rows[2], carried)
    gate_out = head_out.reshape(inner_act.shape) * jax.nn.silu(projected[..., :width_loc])
    tail_rows = tail_inner.shape[0]
    return (gate_out, joined_inner[-tail_rows:], joined_state[-tail_rows:], updated)

def matmul_high(left, right):
    return jnp.dot(left, right, precision=FULL_PRECISION, preferred_element_type=jnp.float32)

def layer(hidden, weights):
    norm_gain, gate_weight, inner_weight, state_weight, step_weight, conv_inner, conv_state, head_params, gate_gain, out_weight = weights
    inv_rms = lax.rsqrt(lax.optimization_barrier(jnp.mean(hidden * hidden, axis=1, keepdims=True)) + EPSILON)
    normed = low(hidden * inv_rms * norm_gain)
    gate_part = low_back(matmul_high(normed, gate_weight))
    inner_part = low_back(matmul_high(normed, inner_weight))
    state_part = low_back(matmul_high(normed, state_weight))
    step_raw = low_back(matmul_high(normed, step_weight))
    projected = jnp.concatenate([gate_part, inner_part, state_part], 1).reshape(MBS, GROUP, 1, 2 * INNER + 2 * STATE)
    raw_blocks = step_raw.reshape(MBS, GROUP, 1, HEADS)

    def advance(carry_state, block_pair):
        tail_inner, tail_state, carried = carry_state
        gate_out, tail_inner, tail_state, carried = mixer_core(block_pair[0], block_pair[1], tail_inner, tail_state, carried, conv_inner, conv_state, head_params)
        return ((tail_inner, tail_state, carried), gate_out)
    initial = (jnp.zeros((CONV - 1, 1, INNER), jnp.float32), jnp.zeros((CONV - 1, 1, 2 * STATE), jnp.float32), jnp.zeros((1, HEADS, HEADDIM, STATE), jnp.float32))
    gate_blocks = lax.scan(jax.checkpoint(advance), initial, (projected, raw_blocks))[1]
    gate_seq = gate_blocks.reshape(LEN, INNER)
    inv_gate = lax.rsqrt(lax.optimization_barrier(jnp.mean(gate_seq * gate_seq, axis=1, keepdims=True)) + EPSILON)
    normed_gate = low(gate_seq * inv_gate * gate_gain)
    return hidden + low_back(matmul_high(normed_gate, out_weight))

def reference(tokens, cotangent, norm_gain, gate_weight, inner_weight, state_weight, step_weight, conv_inner, conv_state, head_params, gate_gain, out_weight):
    weights = tuple((array_in.astype(jnp.float32) for array_in in (norm_gain, gate_weight, inner_weight, state_weight, step_weight, conv_inner, conv_state, head_params, gate_gain, out_weight)))
    inputs = tokens.astype(jnp.float32).reshape(SEQS, LEN, D)
    probe_rows = jnp.zeros((SEQS, LEN, D), jnp.float32)

    def forward(params, probe_in, source):
        first_set = tuple((array_in[0] for array_in in params))
        second_set = tuple((array_in[1] for array_in in params))

        def one_sequence(seq_pair):
            middle = layer(seq_pair[0], first_set)
            return (middle, layer(middle + seq_pair[1], second_set))
        return lax.map(jax.checkpoint(one_sequence), (source, probe_in))
    (middle, final_rows), pullback = jax.vjp(forward, weights, probe_rows, inputs)
    weight_grads, probe_grad, input_part = pullback((jnp.zeros_like(middle), cotangent.astype(jnp.float32).reshape(SEQS, LEN, D)))
    block_shape = (SEQS, MBS, GROUP, D)
    output = jnp.stack([middle.reshape(block_shape), final_rows.reshape(block_shape)])
    input_grad = jnp.stack([input_part.reshape(block_shape), probe_grad.reshape(block_shape)])
    return (output, input_grad, weight_grads[0], weight_grads[1], weight_grads[2], weight_grads[3], weight_grads[4], weight_grads[5], weight_grads[6], weight_grads[7], weight_grads[8], weight_grads[9])
```

```python
import jax
import jax.numpy as jnp
from jax import lax
from jax.sharding import PartitionSpec as P

D = 1024
HEADS = 32
HEADDIM = 64
STATE = 128
CONV = 4
INNER = 2048
CHUNK = 128
SIDE = 128

EPSILON = 1e-05
EXACT = lax.Precision.HIGHEST
FULL_PRECISION = lax.Precision.HIGH
LINK = jnp.float32


def shifted(block, distance):
    route = [(0, 1)] if distance == 1 else [(1, 0)]
    return lax.ppermute(block, "section", route)


def causal_conv(padded, tap_rows):
    rows = padded.shape[1] - CONV + 1
    summed = tap_rows[CONV]
    for offset in range(CONV):
        summed = summed + tap_rows[offset] * padded[:, offset : offset + rows]
    return summed


def with_history(values, tail, first_section, overlap):
    history = jnp.pad(tail, ((0, 0), (overlap - CONV + 1, 0), (0, 0)))
    top = jnp.where(first_section, values[:, :overlap], history)
    return jnp.concatenate([jnp.zeros_like(tail), top, values[:, overlap:]], 1)


def ssd(x_act, b_in, c_out, step, rate, skip):
    seqs, rows, heads = step.shape
    chunks = rows // CHUNK
    x_heads = x_act.reshape(seqs, chunks, CHUNK, heads, HEADDIM)
    b_c = b_in.reshape(seqs, chunks, CHUNK, STATE)
    c_c = c_out.reshape(seqs, chunks, CHUNK, STATE)
    step_c = jnp.transpose(step.reshape(seqs, chunks, CHUNK, heads), (0, 1, 3, 2))
    log_decay = step_c * rate[:, None]
    mask = lax.broadcasted_iota(jnp.int32, (CHUNK, CHUNK), 0) >= lax.broadcasted_iota(
        jnp.int32, (CHUNK, CHUNK), 1
    )
    running = jnp.einsum("bchs,ts->bcht", log_decay, mask.astype(jnp.float32), precision=EXACT)
    total = running[..., -1]
    spread = running[..., :, None] - running[..., None, :]
    kernel = jnp.where(mask, jnp.exp(jnp.where(mask, spread, 0.0)), 0.0)
    weighting = jnp.exp(total[..., None] - running) * step_c
    added = jnp.einsum(
        "bcshp,bcsn->bchpn",
        x_heads * jnp.transpose(weighting, (0, 1, 3, 2))[..., None],
        b_c,
        precision=FULL_PRECISION,
    )
    fade = jnp.exp(total)[..., None, None]
    held = jnp.zeros_like(added[:, 0])
    before = []
    for chunk in range(chunks):
        before.append(held)
        held = fade[:, chunk] * held + added[:, chunk]
    arrived = shifted(held, 1)
    scores = jnp.einsum("bctn,bcsn->bcts", c_c, b_c, precision=FULL_PRECISION)
    mixing = scores[:, :, None] * kernel * step_c[..., None, :]
    inside = jnp.einsum("bchts,bcshp->bcthp", mixing, x_heads, precision=FULL_PRECISION)
    entering = []
    for chunk in range(chunks):
        entering.append(before[chunk] + arrived)
        arrived = fade[:, chunk] * arrived
    carried_out = jnp.einsum(
        "bctn,bchpn->bcthp", c_c, jnp.stack(entering, 1), precision=FULL_PRECISION
    )
    outputs = (
        inside
        + carried_out * jnp.transpose(jnp.exp(running), (0, 1, 3, 2))[..., None]
        + skip[:, None] * x_heads
    )
    return outputs.reshape(x_act.shape)


def mixer(
    gate_part, inner_part, state_part, step_raw, taps_inner, taps_state, head_rows,
    first_section, row_valid, overlap,
):
    tails = shifted(
        jnp.concatenate([inner_part[:, 1 - CONV :], state_part[:, 1 - CONV :]], 2), 1
    )
    width = inner_part.shape[2]
    inner_rows = with_history(inner_part, tails[..., :width], first_section, overlap)
    state_rows = with_history(state_part, tails[..., width:], first_section, overlap)
    x_act = jax.nn.silu(causal_conv(inner_rows, taps_inner))
    state_act = jax.nn.silu(causal_conv(state_rows, taps_state))
    step = jnp.where(row_valid, jax.nn.softplus(step_raw + head_rows[0]), 0.0)
    head_out = ssd(
        x_act,
        state_act[..., :STATE],
        state_act[..., STATE:],
        step,
        -jnp.exp(head_rows[1]),
        head_rows[2],
    )
    return jnp.where(row_valid, head_out * jax.nn.silu(gate_part), 0.0)


def per_device(
    tokens,
    cotangent,
    norm_gain,
    gate_weight,
    inner_weight,
    state_weight,
    step_weight,
    conv_inner,
    conv_state,
    head_params,
    gate_gain,
    out_weight,
):
    tensor_rank = lax.axis_index("tensor")
    section_rank = lax.axis_index("section")
    ranks = lax.axis_size("tensor")
    first_section = section_rank == 0
    seqs, block_count, part_rows, _ = tokens.shape
    held_blocks = (block_count + 1) // 2
    group = part_rows * ranks
    rows = held_blocks * group
    overlap = (2 * held_blocks - block_count) * group
    width = gate_weight.shape[2]
    heads_loc = step_weight.shape[2]
    row_valid = first_section | (
        lax.broadcasted_iota(jnp.int32, (1, rows, 1), 1) >= overlap
    )
    block_valid = first_section | (
        lax.broadcasted_iota(jnp.int32, (1, held_blocks, 1, 1), 1) >= 2 * held_blocks - block_count
    )

    def both_layers(values):
        gathered = lax.all_gather(values, ("section", "dp"), axis=0, tiled=False)
        return gathered.reshape(2, -1, values.shape[-1])

    in_weights = both_layers(
        jnp.concatenate([gate_weight[0], inner_weight[0], state_weight[0], step_weight[0]], 1)
    )
    out_local = lax.dynamic_slice_in_dim(out_weight[0], tensor_rank * width, width, 0)
    out_weights_t = both_layers(out_local.T)
    small_in = lax.all_gather(
        jnp.concatenate(
            [
                norm_gain[0],
                lax.dynamic_slice_in_dim(gate_gain[0], tensor_rank * width, width, 0),
                conv_inner[0].reshape(-1),
                conv_state[0].reshape(-1),
                head_params[0].reshape(-1),
            ]
        ),
        "section",
        axis=0,
        tiled=False,
    )

    def split_small(vector):
        sizes = (
            (D,),
            (width,),
            (CONV + 1, width),
            (CONV + 1, 2 * STATE),
            (3, heads_loc),
        )
        parts, at = [], 0
        for size in sizes:
            count = size[0] * (size[1] if len(size) > 1 else 1)
            parts.append(vector[at : at + count].reshape(size))
            at += count
        return parts

    def spread_rows(values):
        gathered = lax.all_gather(values, "tensor", axis=0, tiled=False)
        return jnp.transpose(gathered, (1, 2, 0, 3, 4)).reshape(seqs, rows, values.shape[-1])

    def by_rank(values):
        split = values.reshape(seqs, held_blocks, ranks, part_rows, values.shape[-1])
        return jnp.transpose(split, (2, 0, 1, 3, 4))

    def row_sums(partial):
        return lax.psum_scatter(
            partial.astype(LINK), "tensor", scatter_dimension=0, tiled=False
        ).astype(jnp.float32)

    def forward(hidden, layer):
        gain_rows, gate_scale, taps_inner, taps_state, head_rows = split_small(small_in[layer])
        proj, out_t = in_weights[layer], out_weights_t[layer]
        inv_rms = lax.rsqrt(jnp.mean(hidden * hidden, axis=3, keepdims=True) + EPSILON)
        normed = spread_rows((hidden * inv_rms * gain_rows).astype(jnp.bfloat16))
        raw = jnp.einsum("btd,dc->btc", normed, proj, preferred_element_type=jnp.float32)
        gate_out, pullback = jax.vjp(
            lambda *parts: mixer(*parts, first_section, row_valid, overlap),
            raw[..., :width],
            raw[..., width : 2 * width],
            raw[..., 2 * width : 2 * width + 2 * STATE],
            raw[..., 2 * width + 2 * STATE :],
            taps_inner,
            taps_state,
            head_rows,
        )
        scaled = (gate_out * gate_scale).astype(jnp.bfloat16)
        partial = jnp.einsum(
            "kbgqc,dc->kbgqd", by_rank(scaled), out_t, preferred_element_type=jnp.float32
        )
        squares = by_rank(jnp.sum(gate_out * gate_out, axis=2, keepdims=True))
        squares = jnp.pad(squares, ((0, 0),) * 4 + ((0, SIDE - 1),))
        summed = row_sums(jnp.concatenate([partial, squares], 4))
        inv_gate = lax.rsqrt(summed[..., D : D + 1] / INNER + EPSILON)
        branch = inv_gate * summed[..., :D]
        kept = (hidden, inv_rms, normed, pullback, gate_out, scaled, inv_gate, branch)
        return hidden + branch, kept

    def backward(grad_out, layer, kept):
        hidden, inv_rms, normed, pullback, gate_out, scaled, inv_gate, branch = kept
        gain_rows, gate_scale = split_small(small_in[layer])[:2]
        proj, out_t = in_weights[layer], out_weights_t[layer]
        pull = inv_gate * inv_gate * jnp.sum(grad_out * branch, axis=3, keepdims=True) / INNER
        pull_high = pull.astype(jnp.bfloat16)
        pull_low = (pull - pull_high.astype(jnp.float32)).astype(jnp.bfloat16)
        side = jnp.pad(
            jnp.concatenate([pull_high, pull_low], 3), ((0, 0),) * 3 + ((0, SIDE - 2),)
        )
        full = spread_rows(
            jnp.concatenate([(inv_gate * grad_out).astype(jnp.bfloat16), side], 3)
        )
        upper = full[..., :D]
        pull_full = full[..., D : D + 1].astype(jnp.float32) + full[..., D + 1 : D + 2].astype(
            jnp.float32
        )
        through = jnp.einsum("btd,dc->btc", upper, out_t, preferred_element_type=jnp.float32)
        out_grad = jnp.einsum("btd,btc->dc", upper, scaled, preferred_element_type=jnp.float32)
        out_grad = lax.psum_scatter(out_grad, "dp", scatter_dimension=0, tiled=True)
        gate_gain_grad = jnp.sum(through * gate_out, axis=(0, 1))
        parts = pullback(gate_scale * through - gate_out * pull_full)
        low = jnp.concatenate([part.astype(jnp.bfloat16) for part in parts[:4]], 2)
        grad_normed = row_sums(
            jnp.einsum("kbgqc,dc->kbgqd", by_rank(low), proj, preferred_element_type=jnp.float32)
        )
        proj_grad = jnp.einsum("btd,btc->dc", normed, low, preferred_element_type=jnp.float32)
        proj_grad = lax.psum_scatter(proj_grad, "dp", scatter_dimension=0, tiled=True)
        norm_gain_grad = jnp.sum(grad_normed * hidden * inv_rms, axis=(0, 1, 2))
        inner_in = jnp.sum(grad_normed * gain_rows * hidden, axis=3, keepdims=True)
        grad_in = grad_out + inv_rms * gain_rows * grad_normed - hidden * inv_rms**3 * inner_in / D
        weight_grads = jnp.concatenate([proj_grad, out_grad], 1)
        shared = jnp.concatenate([norm_gain_grad, parts[5].reshape(-1)])
        own = jnp.concatenate([gate_gain_grad, parts[4].reshape(-1), parts[6].reshape(-1)])
        return grad_in, weight_grads, shared, own

    first_block = jnp.where(first_section, 0, block_count - held_blocks)

    def held(values):
        return lax.dynamic_slice_in_dim(values, first_block, held_blocks, 1)

    extra = 2 * held_blocks - block_count

    def joined(in_first, in_second, to_first, to_second):
        return jnp.where(
            first_section,
            jnp.concatenate([in_first, to_first], 1),
            jnp.concatenate([to_second, in_second[:, extra:]], 1),
        )

    middle, kept_first = forward(held(tokens).astype(jnp.float32), 0)
    final, kept_second = forward(middle, 1)
    output = joined(middle, final, shifted(middle[:, extra:], -1), shifted(final, 1))

    top_grad = jnp.where(block_valid, held(cotangent), 0.0)
    grad_second, weights_second, shared_second, own_second = backward(top_grad, 1, kept_second)
    weights_to_second = shifted(weights_second, 1)
    grad_to_second = shifted(grad_second, 1)
    grad_first, weights_first, shared_first, own_first = backward(grad_second, 0, kept_first)
    weights_to_first = shifted(weights_first, -1)
    input_grad = joined(
        grad_first, grad_second, shifted(grad_first[:, extra:], -1), grad_to_second
    )
    weights = jnp.where(
        first_section, weights_first + weights_to_first, weights_second + weights_to_second
    )
    state_at = 2 * width
    step_at = state_at + 2 * STATE
    out_at = step_at + heads_loc
    state_grad = lax.psum(weights[:, state_at:step_at], "tensor")
    shared = lax.psum(jnp.stack([shared_first, shared_second]), ("section", "dp", "tensor"))
    own = lax.psum(jnp.stack([own_first, own_second]), ("section", "dp"))
    shared = jnp.where(first_section, shared[0], shared[1])
    own = jnp.where(first_section, own[0], own[1])
    taps_end = width * (CONV + 2)
    return (
        output[None],
        input_grad[None],
        shared[:D][None],
        weights[:, :width][None],
        weights[:, width:state_at][None],
        state_grad[None],
        weights[:, step_at:out_at][None],
        own[width:taps_end].reshape(1, CONV + 1, width),
        shared[D:].reshape(1, CONV + 1, 2 * STATE),
        own[taps_end:].reshape(1, 3, heads_loc),
        own[:width][None],
        weights[:, out_at:].T[None],
    )


def solution(mesh):
    return jax.shard_map(
        per_device,
        mesh=mesh,
        in_specs=(
            P("dp", None, "tensor", None),
            P("dp", None, "tensor", None),
            P("section", None),
            P("section", "dp", "tensor"),
            P("section", "dp", "tensor"),
            P("section", "dp", None),
            P("section", "dp", "tensor"),
            P("section", None, "tensor"),
            P("section", None, None),
            P("section", None, "tensor"),
            P("section", None),
            P("section", None, "dp"),
        ),
        out_specs=(
            P("section", "dp", None, "tensor", None),
            P("section", "dp", None, "tensor", None),
            P("section", None),
            P("section", "dp", "tensor"),
            P("section", "dp", "tensor"),
            P("section", "dp", None),
            P("section", "dp", "tensor"),
            P("section", None, "tensor"),
            P("section", None, None),
            P("section", None, "tensor"),
            P("section", "tensor"),
            P("section", "tensor", "dp"),
        ),
        check_vma=False,
    )
```

```python
import jax
import jax.numpy as jnp
from jax import lax
from jax.sharding import PartitionSpec as P

D = 1024
HEADS = 32
HEADDIM = 64
STATE = 128
CONV = 4
INNER = 2048
CHUNK = 128
SIDE = 128

EPSILON = 1e-05
EXACT = lax.Precision.HIGHEST
FULL_PRECISION = lax.Precision.HIGH
LINK = jnp.bfloat16


def shifted(block, distance):
    route = [(0, 1)] if distance == 1 else [(1, 0)]
    return lax.ppermute(block, "section", route)


def swapped(block):
    return lax.ppermute(block, "section", [(0, 1), (1, 0)])


def in_order(values, axis):
    count = lax.axis_size(axis)
    me = lax.axis_index(axis)
    whole = jnp.zeros((count,) + values.shape, values.dtype)
    for step in range(count):
        route = [(i, (i + step) % count) for i in range(count)]
        part = lax.ppermute(values, axis, route) if step else values
        whole = lax.dynamic_update_index_in_dim(whole, part, lax.rem(me + count - step, count), 0)
    return whole


def sum_for_owner(term_for, axis, link):
    count = lax.axis_size(axis)
    me = lax.axis_index(axis)
    arrived = []
    for step in range(1, count):
        route = [(i, (i + step) % count) for i in range(count)]
        term = term_for(lax.rem(me + step, count)).astype(link)
        arrived.append(lax.ppermute(term, axis, route))
    summed = term_for(me)
    for term in arrived:
        summed = summed + term.astype(jnp.float32)
    return summed


def causal_conv(padded, tap_rows):
    rows = padded.shape[1] - CONV + 1
    summed = tap_rows[CONV]
    for offset in range(CONV):
        summed = summed + tap_rows[offset] * padded[:, offset : offset + rows]
    return summed


def with_history(values, tail, first_section, overlap):
    history = jnp.pad(tail, ((0, 0), (overlap - CONV + 1, 0), (0, 0)))
    top = jnp.where(first_section, values[:, :overlap], history)
    return jnp.concatenate([jnp.zeros_like(tail), top, values[:, overlap:]], 1)


def ssd(x_act, b_in, c_out, step, rate, skip):
    seqs, rows, heads = step.shape
    chunks = rows // CHUNK
    x_heads = x_act.reshape(seqs, chunks, CHUNK, heads, HEADDIM)
    b_c = b_in.reshape(seqs, chunks, CHUNK, STATE)
    c_c = c_out.reshape(seqs, chunks, CHUNK, STATE)
    step_c = jnp.transpose(step.reshape(seqs, chunks, CHUNK, heads), (0, 1, 3, 2))
    log_decay = step_c * rate[:, None]
    mask = lax.broadcasted_iota(jnp.int32, (CHUNK, CHUNK), 0) >= lax.broadcasted_iota(
        jnp.int32, (CHUNK, CHUNK), 1
    )
    running = jnp.einsum("bchs,ts->bcht", log_decay, mask.astype(jnp.float32), precision=EXACT)
    total = running[..., -1]
    spread = running[..., :, None] - running[..., None, :]
    kernel = jnp.where(mask, jnp.exp(jnp.where(mask, spread, 0.0)), 0.0)
    weighting = jnp.exp(total[..., None] - running) * step_c
    added = jnp.einsum(
        "bcshp,bcsn->bchpn",
        x_heads * jnp.transpose(weighting, (0, 1, 3, 2))[..., None],
        b_c,
        precision=FULL_PRECISION,
    )
    fade = jnp.exp(total)[..., None, None]
    held = jnp.zeros_like(added[:, 0])
    before = []
    for chunk in range(chunks):
        before.append(held)
        held = fade[:, chunk] * held + added[:, chunk]
    arrived = shifted(held, 1)
    scores = jnp.einsum("bctn,bcsn->bcts", c_c, b_c, precision=FULL_PRECISION)
    mixing = scores[:, :, None] * kernel * step_c[..., None, :]
    inside = jnp.einsum("bchts,bcshp->bcthp", mixing, x_heads, precision=FULL_PRECISION)
    entering = []
    for chunk in range(chunks):
        entering.append(before[chunk] + arrived)
        arrived = fade[:, chunk] * arrived
    carried_out = jnp.einsum(
        "bctn,bchpn->bcthp", c_c, jnp.stack(entering, 1), precision=FULL_PRECISION
    )
    outputs = (
        inside
        + carried_out * jnp.transpose(jnp.exp(running), (0, 1, 3, 2))[..., None]
        + skip[:, None] * x_heads
    )
    return outputs.reshape(x_act.shape)


def mixer(
    gate_part, inner_part, state_part, step_raw, taps_inner, taps_state, head_rows,
    first_section, row_valid, overlap,
):
    tails = shifted(
        jnp.concatenate([inner_part[:, 1 - CONV :], state_part[:, 1 - CONV :]], 2), 1
    )
    width = inner_part.shape[2]
    inner_rows = with_history(inner_part, tails[..., :width], first_section, overlap)
    state_rows = with_history(state_part, tails[..., width:], first_section, overlap)
    x_act = jax.nn.silu(causal_conv(inner_rows, taps_inner))
    state_act = jax.nn.silu(causal_conv(state_rows, taps_state))
    step = jnp.where(row_valid, jax.nn.softplus(step_raw + head_rows[0]), 0.0)
    head_out = ssd(
        x_act,
        state_act[..., :STATE],
        state_act[..., STATE:],
        step,
        -jnp.exp(head_rows[1]),
        head_rows[2],
    )
    return jnp.where(row_valid, head_out * jax.nn.silu(gate_part), 0.0)


def per_device(
    tokens,
    cotangent,
    norm_gain,
    gate_weight,
    inner_weight,
    state_weight,
    step_weight,
    conv_inner,
    conv_state,
    head_params,
    gate_gain,
    out_weight,
):
    tensor_rank = lax.axis_index("tensor")
    section_rank = lax.axis_index("section")
    ranks = lax.axis_size("tensor")
    first_section = section_rank == 0
    seqs, block_count, part_rows, _ = tokens.shape
    held_blocks = (block_count + 1) // 2
    group = part_rows * ranks
    rows = held_blocks * group
    overlap = (2 * held_blocks - block_count) * group
    width = gate_weight.shape[2]
    heads_loc = step_weight.shape[2]
    row_valid = first_section | (
        lax.broadcasted_iota(jnp.int32, (1, rows, 1), 1) >= overlap
    )
    block_valid = first_section | (
        lax.broadcasted_iota(jnp.int32, (1, held_blocks, 1, 1), 1) >= 2 * held_blocks - block_count
    )

    def both_layers(values):
        gathered = lax.all_gather(values, ("section", "dp"), axis=0, tiled=False)
        return gathered.reshape(2, -1, values.shape[-1])

    in_weights = both_layers(
        jnp.concatenate([gate_weight[0], inner_weight[0], state_weight[0], step_weight[0]], 1)
    )
    out_local = lax.dynamic_slice_in_dim(out_weight[0], tensor_rank * width, width, 0)
    out_weights_t = both_layers(out_local.T)
    own_small = jnp.concatenate(
        [
            norm_gain[0],
            lax.dynamic_slice_in_dim(gate_gain[0], tensor_rank * width, width, 0),
            conv_inner[0].reshape(-1),
            conv_state[0].reshape(-1),
            head_params[0].reshape(-1),
        ]
    )
    other_small = swapped(own_small)
    small_in = (
        jnp.where(first_section, own_small, other_small),
        jnp.where(first_section, other_small, own_small),
    )

    def split_small(vector):
        sizes = (
            (D,),
            (width,),
            (CONV + 1, width),
            (CONV + 1, 2 * STATE),
            (3, heads_loc),
        )
        parts, at = [], 0
        for size in sizes:
            count = size[0] * (size[1] if len(size) > 1 else 1)
            parts.append(vector[at : at + count].reshape(size))
            at += count
        return parts

    def spread_rows(values):
        columns = values.shape[-1]
        whole = jnp.zeros((seqs, held_blocks, ranks, part_rows, columns), values.dtype)
        for step in range(ranks):
            route = [(i, (i + step) % ranks) for i in range(ranks)]
            part = lax.ppermute(values, "tensor", route) if step else values
            source = lax.rem(tensor_rank + ranks - step, ranks)
            whole = lax.dynamic_update_slice_in_dim(whole, part[:, :, None], source, 2)
        return whole.reshape(seqs, rows, columns)

    def rows_of(values, rank):
        split = values.reshape(seqs, held_blocks, ranks, part_rows, values.shape[-1])
        return lax.dynamic_index_in_dim(split, rank, 2, keepdims=False)

    def row_sums(values, weights):
        def term_for(rank):
            return jnp.einsum(
                "bgqc,dc->bgqd", rows_of(values, rank), weights, preferred_element_type=jnp.float32
            )

        return sum_for_owner(term_for, "tensor", LINK)

    shard = gate_weight.shape[1]

    def weight_sums(left, right):
        def term_for(rank):
            part = lax.dynamic_slice_in_dim(left, rank * shard, shard, 2)
            return jnp.einsum("btd,btc->dc", part, right, preferred_element_type=jnp.float32)

        return sum_for_owner(term_for, "dp", LINK)

    def forward(hidden, layer):
        gain_rows, gate_scale, taps_inner, taps_state, head_rows = split_small(small_in[layer])
        proj, out_t = in_weights[layer], out_weights_t[layer]
        inv_rms = lax.rsqrt(jnp.mean(hidden * hidden, axis=3, keepdims=True) + EPSILON)
        normed = spread_rows((hidden * inv_rms * gain_rows).astype(jnp.bfloat16))
        raw = jnp.einsum("btd,dc->btc", normed, proj, preferred_element_type=jnp.float32)
        gate_out, pullback = jax.vjp(
            lambda *parts: mixer(*parts, first_section, row_valid, overlap),
            raw[..., :width],
            raw[..., width : 2 * width],
            raw[..., 2 * width : 2 * width + 2 * STATE],
            raw[..., 2 * width + 2 * STATE :],
            taps_inner,
            taps_state,
            head_rows,
        )
        scaled = (gate_out * gate_scale).astype(jnp.bfloat16)
        squares = jnp.sum(gate_out * gate_out, axis=2, keepdims=True)
        squares = sum_for_owner(
            lambda rank: rows_of(squares, rank)[..., 0], "tensor", jnp.float32
        )
        inv_gate = lax.rsqrt(squares / INNER + EPSILON)[..., None]
        branch = inv_gate * row_sums(scaled, out_t)
        kept = (hidden, inv_rms, normed, pullback, gate_out, scaled, inv_gate, branch)
        return hidden + branch, kept

    def backward(grad_out, layer, kept):
        hidden, inv_rms, normed, pullback, gate_out, scaled, inv_gate, branch = kept
        gain_rows, gate_scale = split_small(small_in[layer])[:2]
        proj, out_t = in_weights[layer], out_weights_t[layer]
        pull = inv_gate * inv_gate * jnp.sum(grad_out * branch, axis=3, keepdims=True) / INNER
        pull_high = pull.astype(jnp.bfloat16)
        pull_low = (pull - pull_high.astype(jnp.float32)).astype(jnp.bfloat16)
        side = jnp.pad(
            jnp.concatenate([pull_high, pull_low], 3), ((0, 0),) * 3 + ((0, SIDE - 2),)
        )
        full = spread_rows(
            jnp.concatenate([(inv_gate * grad_out).astype(jnp.bfloat16), side], 3)
        )
        upper = full[..., :D]
        pull_full = full[..., D : D + 1].astype(jnp.float32) + full[..., D + 1 : D + 2].astype(
            jnp.float32
        )
        through = jnp.einsum("btd,dc->btc", upper, out_t, preferred_element_type=jnp.float32)
        out_grad = weight_sums(upper, scaled)
        gate_gain_grad = jnp.sum(through * gate_out, axis=(0, 1))
        parts = pullback(gate_scale * through - gate_out * pull_full)
        low = jnp.concatenate([part.astype(jnp.bfloat16) for part in parts[:4]], 2)
        grad_normed = row_sums(low, proj)
        proj_grad = weight_sums(normed, low)
        norm_gain_grad = jnp.sum(grad_normed * hidden * inv_rms, axis=(0, 1, 2))
        inner_in = jnp.sum(grad_normed * gain_rows * hidden, axis=3, keepdims=True)
        grad_in = grad_out + inv_rms * gain_rows * grad_normed - hidden * inv_rms**3 * inner_in / D
        weight_grads = jnp.concatenate([proj_grad, out_grad], 1)
        shared = jnp.concatenate([norm_gain_grad, parts[5].reshape(-1)])
        own = jnp.concatenate([gate_gain_grad, parts[4].reshape(-1), parts[6].reshape(-1)])
        return grad_in, weight_grads, shared, own

    first_block = jnp.where(first_section, 0, block_count - held_blocks)

    def held(values):
        return lax.dynamic_slice_in_dim(values, first_block, held_blocks, 1)

    extra = 2 * held_blocks - block_count

    def joined(in_first, in_second, to_first, to_second):
        return jnp.where(
            first_section,
            jnp.concatenate([in_first, to_first], 1),
            jnp.concatenate([to_second, in_second[:, extra:]], 1),
        )

    middle, kept_first = forward(held(tokens).astype(jnp.float32), 0)
    final, kept_second = forward(middle, 1)
    output = joined(middle, final, shifted(middle[:, extra:], -1), shifted(final, 1))

    top_grad = jnp.where(block_valid, held(cotangent), 0.0)
    grad_second, weights_second, shared_second, own_second = backward(top_grad, 1, kept_second)
    weights_to_second = shifted(weights_second.astype(LINK), 1).astype(jnp.float32)
    grad_to_second = shifted(grad_second, 1)
    grad_first, weights_first, shared_first, own_first = backward(grad_second, 0, kept_first)
    weights_to_first = shifted(weights_first.astype(LINK), -1).astype(jnp.float32)
    input_grad = joined(
        grad_first, grad_second, shifted(grad_first[:, extra:], -1), grad_to_second
    )
    weights = jnp.where(
        first_section, weights_first + weights_to_first, weights_second + weights_to_second
    )
    state_at = 2 * width
    step_at = state_at + 2 * STATE
    out_at = step_at + heads_loc
    small_first = jnp.sum(in_order(jnp.concatenate([shared_first, own_first]), "dp"), axis=0)
    small_second = jnp.sum(in_order(jnp.concatenate([shared_second, own_second]), "dp"), axis=0)
    small = jnp.where(first_section, small_first, small_second) + swapped(
        jnp.where(first_section, small_second, small_first)
    )
    shared_count = shared_first.shape[0]
    own = small[shared_count:]
    over_heads = jnp.concatenate(
        [weights[:, state_at:step_at].reshape(-1), small[:shared_count]]
    ).astype(LINK)
    over_heads = jnp.sum(in_order(over_heads, "tensor").astype(jnp.float32), axis=0)
    state_grad = over_heads[:-shared_count].reshape(shard, 2 * STATE)
    shared = over_heads[-shared_count:]
    taps_end = width * (CONV + 2)
    return (
        output[None],
        input_grad[None],
        shared[:D][None],
        weights[:, :width][None],
        weights[:, width:state_at][None],
        state_grad[None],
        weights[:, step_at:out_at][None],
        own[width:taps_end].reshape(1, CONV + 1, width),
        shared[D:].reshape(1, CONV + 1, 2 * STATE),
        own[taps_end:].reshape(1, 3, heads_loc),
        own[:width][None],
        weights[:, out_at:].T[None],
    )


def solution(mesh):
    return jax.shard_map(
        per_device,
        mesh=mesh,
        in_specs=(
            P("dp", None, "tensor", None),
            P("dp", None, "tensor", None),
            P("section", None),
            P("section", "dp", "tensor"),
            P("section", "dp", "tensor"),
            P("section", "dp", None),
            P("section", "dp", "tensor"),
            P("section", None, "tensor"),
            P("section", None, None),
            P("section", None, "tensor"),
            P("section", None),
            P("section", None, "dp"),
        ),
        out_specs=(
            P("section", "dp", None, "tensor", None),
            P("section", "dp", None, "tensor", None),
            P("section", None),
            P("section", "dp", "tensor"),
            P("section", "dp", "tensor"),
            P("section", "dp", None),
            P("section", "dp", "tensor"),
            P("section", None, "tensor"),
            P("section", None, None),
            P("section", None, "tensor"),
            P("section", "tensor"),
            P("section", "tensor", "dp"),
        ),
        check_vma=False,
    )
```
